32 devices in a mesh: gx: 8 (over z, x), gy: 4 (over y, core).
Axes of the slice: x: 2, y: 2, z: 4, core: 2. Of those that a mesh axis runs over, the one named last changes fastest.
Arguments:
- field: bfloat16 [20, 128, 128, 1024], P(None, 'gx', 'gy'), may hold values from -6 to 6
- cotangent: bfloat16 [20, 128, 128, 1024], P(None, 'gx', 'gy'), may hold values from -6 to 6
- spectral_weight: bfloat16 [2, 20, 20, 24, 4608], P(None, None, None, None, ('gy', 'gx')), may hold values from -30 to 30
- local_weight: bfloat16 [20, 20], replicated, may hold values from -1.25 to 1.25
- bias: float32 [20], replicated, may hold values from -4 to 4
Outputs:
- grad_field: bfloat16 [20, 128, 128, 1024], P(None, 'gx', 'gy')
- grad_weight: float32 [2, 20, 20, 24, 4608], P(None, None, None, None, ('gy', 'gx'))
The draws below stay inside these ranges and needn't reach their ends.
All inputs are finite; a program needn't handle non-finite values.
Results may differ from the reference program's by a relative error of at most 0.03.
Values may be sent and summed in bfloat16 or wider, within the bound.
A program may use at most 256 MiB of HBM per device.

```python
import math
import jax
import jax.numpy as jnp
from jax import lax

C = 20
NX = 128
NY = 128
NZ = 128
NT = 8
MS = 24
MT = 8


def draw_spectral_weight(key, part):
    scale_key, value_key = jax.random.split(jax.random.fold_in(key, 17))
    shape = (2, C, C, MS, MS * MS * MT)
    logs = jax.random.uniform(scale_key, (MS * MS * MT,), jnp.float32, math.log(0.2), math.log(5.0))
    scales = jnp.exp(logs)
    base = jnp.clip(jax.random.normal(value_key, shape, jnp.float32), -3.0, 3.0)
    return (2.0 * base * scales).astype(jnp.bfloat16)


def level_of(own_key, shape, pieces, low, high):
    factor_of, own = 1.0, jax.random.fold_in(own_key, 6)
    for axis_at, shards_of in pieces:
        heights = jnp.exp(jax.random.uniform(jax.random.fold_in(own, axis_at), (shards_of,), jnp.float32, low / len(pieces), high / len(pieces)))
        factor_of = factor_of * jnp.repeat(heights, shape[axis_at] // shards_of).reshape([-1 if axis == axis_at else 1 for axis in range(len(shape))])
    return factor_of


def bell_draw(key, extent, width, limit, pieces=(), kind=jnp.bfloat16):
    loudness = level_of(key, extent, pieces, -0.22, 0.18) if pieces else 1.0
    values = jax.random.normal(key, extent, jnp.float32) * width * loudness
    return jnp.minimum(jnp.maximum(values, -limit), limit).astype(kind)


def setup_inputs(seed: int = 0) -> dict:
    keys = jax.random.split(jax.random.key(seed), 6)
    field = bell_draw(keys[0], (C, NX, NY, NZ * NT), 1.0, 6.0, ((1, 8), (2, 4)))
    cotangent = bell_draw(keys[1], (C, NX, NY, NZ * NT), 1.0, 6.0, ((1, 8), (2, 4)))
    spectral_weight = draw_spectral_weight(jax.random.fold_in(keys[5], 71), 0)
    local_weight = bell_draw(keys[3], (C, C), C ** -0.5, 1.25)
    bias = bell_draw(keys[4], (C,), 1.0, 4.0, (), jnp.float32)
    return {"field": field, "cotangent": cotangent, "spectral_weight": spectral_weight, "local_weight": local_weight, "bias": bias}


def axis_tables(length, kept_count, positions):
    half_kept = kept_count // 2
    mode_index = jnp.arange(kept_count, dtype=jnp.int32)
    frequency = jnp.where(mode_index < half_kept, mode_index, mode_index - kept_count)
    phases = jnp.mod(frequency[:, None] * positions[None, :].astype(jnp.int32), length)
    angles = phases.astype(jnp.float32) * (2.0 * math.pi / length)
    factor = 1.0 / math.sqrt(length)
    return ((jnp.cos(angles) * factor).astype(jnp.bfloat16), (jnp.sin(angles) * factor).astype(jnp.bfloat16))

def plane_tables(depth_cells, time_steps, kept_count, kept_time):
    period = depth_cells * time_steps
    positions = jnp.arange(period, dtype=jnp.int32)
    depth_pos = positions // time_steps
    time_pos = positions % time_steps
    mode_index = jnp.arange(kept_count * kept_time, dtype=jnp.int32)
    space_index = mode_index // kept_time
    time_index = mode_index % kept_time
    frequency = jnp.where(space_index < kept_count // 2, space_index, space_index - kept_count)
    phase_depth = jnp.mod(depth_pos[:, None] * frequency[None, :], depth_cells)
    phase_time = jnp.mod(time_pos[:, None] * time_index[None, :], time_steps)
    phases = jnp.mod(phase_depth * time_steps + phase_time * depth_cells, period)
    angles = phases.astype(jnp.float32) * (2.0 * math.pi / period)
    factor = 1.0 / math.sqrt(period)
    return jnp.concatenate([jnp.cos(angles) * factor, -jnp.sin(angles) * factor], axis=1).astype(jnp.bfloat16)

def forward_axis(values, cos_table, sin_table):
    values = values.astype(jnp.float32)
    with_cos = jnp.einsum('kn,lnrm->lrkm', cos_table.astype(jnp.float32), values)
    with_sin = jnp.einsum('kn,lnrm->lrkm', sin_table.astype(jnp.float32), values)
    real_part = with_cos[:, 0] + with_sin[:, 1]
    imag_part = with_cos[:, 1] - with_sin[:, 0]
    return jnp.stack([real_part, imag_part], axis=1)

def inverse_axis(values, cos_table, sin_table):
    values = values.astype(jnp.float32)
    with_cos = jnp.einsum('kn,lrkm->lnrm', cos_table.astype(jnp.float32), values)
    with_sin = jnp.einsum('kn,lrkm->lnrm', sin_table.astype(jnp.float32), values)
    real_part = with_cos[:, :, 0] - with_sin[:, :, 1]
    imag_part = with_cos[:, :, 1] + with_sin[:, :, 0]
    return jnp.stack([real_part, imag_part], axis=2)

def spectral_apply(weights, mode_values):
    real_weight = weights[0].astype(jnp.float32)
    imag_weight = weights[1].astype(jnp.float32)
    real_mode = mode_values[:, 0].astype(jnp.float32)
    imag_mode = mode_values[:, 1].astype(jnp.float32)
    out_real = jnp.einsum('iokm,ikm->okm', real_weight, real_mode) - jnp.einsum('iokm,ikm->okm', imag_weight, imag_mode)
    out_imag = jnp.einsum('iokm,ikm->okm', real_weight, imag_mode) + jnp.einsum('iokm,ikm->okm', imag_weight, real_mode)
    return jnp.stack([out_real, out_imag], axis=1).astype(jnp.bfloat16)

def spectral_adjoint(weights, mode_values, upstream_modes):
    real_weight = weights[0].astype(jnp.float32)
    imag_weight = weights[1].astype(jnp.float32)
    real_mode = mode_values[:, 0].astype(jnp.float32)
    imag_mode = mode_values[:, 1].astype(jnp.float32)
    real_up = upstream_modes[:, 0].astype(jnp.float32)
    imag_up = upstream_modes[:, 1].astype(jnp.float32)
    grad_real = real_up[None] * real_mode[:, None] + imag_up[None] * imag_mode[:, None]
    grad_imag = imag_up[None] * real_mode[:, None] - real_up[None] * imag_mode[:, None]
    back_real = jnp.einsum('iokm,okm->ikm', real_weight, real_up) + jnp.einsum('iokm,okm->ikm', imag_weight, imag_up)
    back_imag = jnp.einsum('iokm,okm->ikm', real_weight, imag_up) - jnp.einsum('iokm,okm->ikm', imag_weight, real_up)
    return (jnp.stack([grad_real, grad_imag], axis=0), jnp.stack([back_real, back_imag], axis=1))

def gelu_slope(values):
    return 0.5 * (1.0 + lax.erf(values * 0.7071067811865476)) + values * jnp.exp(-0.5 * values * values) * 0.3989422804014327

def reference(field, cotangent, spectral_weight, local_weight, bias):
    kept_plane = MS * MT
    plane_table = plane_tables(NZ, NT, MS, MT)
    cos_wide, sin_wide = axis_tables(NY, MS, jnp.arange(NY, dtype=jnp.int32))
    cos_across, sin_across = axis_tables(NX, MS, jnp.arange(NX, dtype=jnp.int32))
    local_float = local_weight.astype(jnp.float32)

    def first_step(planes):
        product = jnp.dot(planes.reshape(-1, NZ * NT), plane_table, preferred_element_type=jnp.float32)
        return product.astype(jnp.bfloat16)

    def forward_chain(moved):
        coeffs = lax.map(first_step, moved).reshape(NX * C, NY, 2, kept_plane)
        row_modes = forward_axis(coeffs, cos_wide, sin_wide).astype(jnp.bfloat16)
        row_modes = row_modes.reshape(NX, C, 2, MS * kept_plane).transpose(1, 0, 2, 3)
        return forward_axis(row_modes, cos_across, sin_across).astype(jnp.bfloat16)

    def inverse_chain(mode_values):
        across = inverse_axis(mode_values, cos_across, sin_across).astype(jnp.bfloat16)
        row_modes = across.transpose(1, 0, 2, 3).reshape(NX * C, 2, MS, kept_plane)
        cell_modes = inverse_axis(row_modes, cos_wide, sin_wide).astype(jnp.bfloat16)
        return cell_modes.reshape(NX, C * NY, 2 * kept_plane)

    def last_step(cell_modes):
        summed = lax.dot_general(cell_modes, plane_table, (((1,), (1,)), ((), ())), preferred_element_type=jnp.float32)
        return summed.reshape(C, NY, NZ * NT)
    moved_field = jnp.moveaxis(field, 1, 0)
    moved_cot = jnp.moveaxis(cotangent, 1, 0)
    field_modes = forward_chain(moved_field)
    mixed_modes = spectral_apply(spectral_weight, field_modes)
    joined = inverse_chain(mixed_modes)

    def activate(inputs):
        cell_modes, planes, cot_planes = inputs
        direct = jnp.einsum('io,iyp->oyp', local_float, planes.astype(jnp.float32))
        before = last_step(cell_modes) + direct + bias.astype(jnp.float32)[:, None, None]
        return (cot_planes.astype(jnp.float32) * gelu_slope(before)).astype(jnp.bfloat16)
    upstream = lax.map(activate, (joined, moved_field, moved_cot))
    upstream_modes = forward_chain(upstream)
    grad_weight, back_modes = spectral_adjoint(spectral_weight, field_modes, upstream_modes)
    back_joined = inverse_chain(back_modes.astype(jnp.bfloat16))

    def finish(inputs):
        cell_modes, up_planes = inputs
        direct = jnp.einsum('io,oyp->iyp', local_float, up_planes.astype(jnp.float32))
        return (last_step(cell_modes) + direct).astype(jnp.bfloat16)
    result = lax.map(finish, (back_joined, upstream))
    return (jnp.moveaxis(result, 0, 1), grad_weight)
```

```python
import functools
import math

import jax
import jax.numpy as jnp
from jax import lax
from jax.experimental import pallas as pl
from jax.experimental.pallas import tpu as pltpu
from jax.sharding import PartitionSpec as P

NX = 128
NY = 128
NZ = 128
NT = 8
MS = 24
MT = 8


def axis_tables(length, kept_count, positions):
    half_kept = kept_count // 2
    mode_index = jnp.arange(kept_count, dtype=jnp.int32)
    frequency = jnp.where(mode_index < half_kept, mode_index, mode_index - kept_count)
    phases = jnp.mod(frequency[:, None] * positions[None, :], length)
    angles = phases.astype(jnp.float32) * (2.0 * math.pi / length)
    factor = 1.0 / math.sqrt(length)
    return (
        (jnp.cos(angles) * factor).astype(jnp.bfloat16),
        (jnp.sin(angles) * factor).astype(jnp.bfloat16),
    )


def plane_tables(depth_cells, time_steps, kept_count, kept_time):
    period = depth_cells * time_steps
    positions = jnp.arange(period, dtype=jnp.int32)
    depth_pos = positions // time_steps
    time_pos = positions % time_steps
    mode_index = jnp.arange(kept_count * kept_time, dtype=jnp.int32)
    space_index = mode_index // kept_time
    time_index = mode_index % kept_time
    frequency = jnp.where(space_index < kept_count // 2, space_index, space_index - kept_count)
    phase_depth = jnp.mod(depth_pos[:, None] * frequency[None, :], depth_cells)
    phase_time = jnp.mod(time_pos[:, None] * time_index[None, :], time_steps)
    phases = jnp.mod(phase_depth * time_steps + phase_time * depth_cells, period)
    angles = phases.astype(jnp.float32) * (2.0 * math.pi / period)
    factor = 1.0 / math.sqrt(period)
    return jnp.concatenate([jnp.cos(angles) * factor, -jnp.sin(angles) * factor], axis=1).astype(
        jnp.bfloat16
    )


def forward_axis(values, cos_table, sin_table):
    with_cos = jnp.einsum("kn,lnrm->lrkm", cos_table, values, preferred_element_type=jnp.float32)
    with_sin = jnp.einsum("kn,lnrm->lrkm", sin_table, values, preferred_element_type=jnp.float32)
    real_part = with_cos[:, 0] + with_sin[:, 1]
    imag_part = with_cos[:, 1] - with_sin[:, 0]
    return jnp.stack([real_part, imag_part], axis=1)


def inverse_axis(values, cos_table, sin_table):
    with_cos = jnp.einsum("kn,lrkm->lnrm", cos_table, values, preferred_element_type=jnp.float32)
    with_sin = jnp.einsum("kn,lrkm->lnrm", sin_table, values, preferred_element_type=jnp.float32)
    real_part = with_cos[:, :, 0] - with_sin[:, :, 1]
    imag_part = with_cos[:, :, 1] + with_sin[:, :, 0]
    return jnp.stack([real_part, imag_part], axis=2)


def spectral_apply(weights, mode_values):
    real_weight, imag_weight = (weights[0], weights[1])
    real_mode, imag_mode = (mode_values[:, 0], mode_values[:, 1])
    out_real = jnp.einsum(
        "iokm,ikm->okm", real_weight, real_mode, preferred_element_type=jnp.float32
    ) - jnp.einsum("iokm,ikm->okm", imag_weight, imag_mode, preferred_element_type=jnp.float32)
    out_imag = jnp.einsum(
        "iokm,ikm->okm", real_weight, imag_mode, preferred_element_type=jnp.float32
    ) + jnp.einsum("iokm,ikm->okm", imag_weight, real_mode, preferred_element_type=jnp.float32)
    return jnp.stack([out_real, out_imag], axis=1).astype(jnp.bfloat16)


def spectral_adjoint(weights, mode_values, upstream_modes):
    real_weight, imag_weight = (weights[0], weights[1])
    real_mode = mode_values[:, 0].astype(jnp.float32)
    imag_mode = mode_values[:, 1].astype(jnp.float32)
    real_up = upstream_modes[:, 0].astype(jnp.float32)
    imag_up = upstream_modes[:, 1].astype(jnp.float32)
    grad_real = real_up[None] * real_mode[:, None] + imag_up[None] * imag_mode[:, None]
    grad_imag = imag_up[None] * real_mode[:, None] - real_up[None] * imag_mode[:, None]
    real_low = upstream_modes[:, 0]
    imag_low = upstream_modes[:, 1]
    back_real = jnp.einsum(
        "iokm,okm->ikm", real_weight, real_low, preferred_element_type=jnp.float32
    ) + jnp.einsum("iokm,okm->ikm", imag_weight, imag_low, preferred_element_type=jnp.float32)
    back_imag = jnp.einsum(
        "iokm,okm->ikm", real_weight, imag_low, preferred_element_type=jnp.float32
    ) - jnp.einsum("iokm,okm->ikm", imag_weight, real_low, preferred_element_type=jnp.float32)
    return (jnp.stack([grad_real, grad_imag], axis=0), jnp.stack([back_real, back_imag], axis=1))


def gelu_slope(values):
    return (
        0.5 * (1.0 + lax.erf(values * 0.7071067811865476))
        + values * jnp.exp(-0.5 * values * values) * 0.3989422804014327
    )


def local(field, cotangent, spectral_weight, local_weight, bias):
    channels, width_x, width_y, depth_cells = field.shape
    kept_plane = MS * MT
    plane_table = plane_tables(NZ, NT, MS, MT)
    local_rows = lax.axis_index("gy") * width_y + jnp.arange(width_y, dtype=jnp.int32)
    cos_local, sin_local = axis_tables(NY, MS, local_rows)
    cos_across, sin_across = axis_tables(NX, MS, jnp.arange(NX, dtype=jnp.int32))

    def forward_chain(planes):
        coeffs = jnp.dot(
            planes.reshape(-1, depth_cells), plane_table, preferred_element_type=jnp.float32
        )
        coeffs = coeffs.astype(jnp.bfloat16).reshape(channels * width_x, width_y, 2, kept_plane)
        partial_terms = forward_axis(coeffs, cos_local, sin_local)
        row_modes = lax.psum_scatter(
            partial_terms.astype(jnp.bfloat16), "gy", scatter_dimension=2, tiled=True
        )
        row_modes = row_modes.reshape(channels, width_x, 2, -1)
        blocks = lax.all_to_all(row_modes, "gx", split_axis=3, concat_axis=1, tiled=True)
        return forward_axis(blocks, cos_across, sin_across).astype(jnp.bfloat16)

    def inverse_chain(mode_values):
        across = inverse_axis(mode_values, cos_across, sin_across).astype(jnp.bfloat16)
        row_modes = lax.all_to_all(across, "gx", split_axis=1, concat_axis=3, tiled=True)
        row_modes = row_modes.reshape(channels * width_x, 2, -1, kept_plane)
        all_rows = lax.all_gather(row_modes, "gy", axis=2, tiled=True)
        cell_modes = inverse_axis(all_rows, cos_local, sin_local).astype(jnp.bfloat16)
        flattened = cell_modes.reshape(-1, 2 * kept_plane)
        summed = lax.dot_general(
            flattened, plane_table, (((1,), (1,)), ((), ())), preferred_element_type=jnp.float32
        )
        return summed.reshape(field.shape)

    field_modes = forward_chain(field)
    mixed_modes = spectral_apply(spectral_weight, field_modes)
    spectral = inverse_chain(mixed_modes)
    direct = jnp.einsum("io,ixyp->oxyp", local_weight, field, preferred_element_type=jnp.float32)
    before = spectral + direct + bias[:, None, None, None]
    upstream = (cotangent.astype(jnp.float32) * gelu_slope(before)).astype(jnp.bfloat16)
    upstream_modes = forward_chain(upstream)
    grad_weight, back_modes = spectral_adjoint(spectral_weight, field_modes, upstream_modes)
    returned = inverse_chain(back_modes.astype(jnp.bfloat16))
    direct_back = jnp.einsum(
        "io,oxyp->ixyp", local_weight, upstream, preferred_element_type=jnp.float32
    )
    return ((returned + direct_back).astype(jnp.bfloat16), grad_weight)


def kernel_tables(width_x, gx_size):
    group = lax.axis_index("gy")
    share = MS // 4
    order = jnp.array([0, 2, 1, 3], dtype=jnp.int32)
    owners = jnp.bitwise_xor(group, order)
    kept_rows = (owners[:, None] * share + jnp.arange(share, dtype=jnp.int32)[None, :]).reshape(-1)
    cells = NY // 4
    local_rows = group * cells + jnp.arange(cells, dtype=jnp.int32)
    cos_rows, sin_rows = axis_tables(NY, MS, local_rows)
    eye_x = jnp.eye(8, dtype=jnp.bfloat16)

    def spread(table):
        table = jnp.take(table, kept_rows, axis=0)
        return (table[:, None, None, :] * eye_x[None, :, :, None]).reshape(MS * 8, 8 * cells)

    row_table = jnp.concatenate([spread(cos_rows), spread(sin_rows)], axis=0)
    cos_x, sin_x = axis_tables(NX, MS, jnp.arange(NX, dtype=jnp.int32))
    parts = jnp.stack(
        [jnp.stack([cos_x, sin_x], axis=0), jnp.stack([-sin_x, cos_x], axis=0)], axis=0
    ).reshape(2, 2, MS, gx_size, width_x)
    eye_c = jnp.eye(4, dtype=jnp.bfloat16)
    across = parts.transpose(0, 2, 3, 1, 4)[:, None, :, :, :, None, :] * eye_c[
        None, :, None, None, None, :, None
    ]
    return row_table, across.reshape(2 * 4 * MS, gx_size * 2 * 4 * width_x)


def params(semantics=("arbitrary",)):
    return pltpu.CompilerParams(dimension_semantics=semantics, vmem_limit_bytes=56 * 1024 * 1024)


def whole(shape):
    return pl.BlockSpec(shape, lambda *_: (0,) * len(shape))


def rows_kernel(planes_ref, plane_ref, row_ref, near_ref, far_ref):
    count, width_x, cells, depth = planes_ref.shape
    kept = MS * MT
    rows = 8 * cells
    half = MS // 2
    for c in range(count):
        pieces = []
        for g in range(width_x // 8):
            seg = planes_ref[c, g * 8 : g * 8 + 8].reshape(rows, depth)
            modes = jnp.dot(seg, plane_ref[...], preferred_element_type=jnp.float32)
            both = jnp.dot(
                row_ref[...], modes.astype(jnp.bfloat16), preferred_element_type=jnp.float32
            )
            top, low = both[: MS * 8], both[MS * 8 :]
            real = top[:, :kept] + low[:, 256 : 256 + kept]
            imag = top[:, 256 : 256 + kept] - low[:, :kept]
            pieces.append(jnp.concatenate([real, imag], axis=1).reshape(MS, 8, 2 * kept))
        out = jnp.concatenate(pieces, axis=1).astype(jnp.bfloat16)
        near_ref[:, c] = out[:half]
        far_ref[:, c] = out[half:]


def rows_call(planes, first, count, plane_pad, row_table):
    _, width_x, cells, depth = planes.shape
    step = 2
    kept = MS * MT
    half = MS // 2
    out = jax.ShapeDtypeStruct((half, count, width_x, 2 * kept), jnp.bfloat16)
    block = pl.BlockSpec((half, step, width_x, 2 * kept), lambda s: (0, s, 0, 0))
    flops = 2 * count * width_x * cells * depth * 2 * kept
    return pl.pallas_call(
        rows_kernel,
        grid=(count // step,),
        in_specs=[
            pl.BlockSpec((step, width_x, cells, depth), lambda s: (first // step + s, 0, 0, 0)),
            whole(plane_pad.shape),
            whole(row_table.shape),
        ],
        out_specs=[block, block],
        out_shape=[out, out],
        compiler_params=params(),
        cost_estimate=pl.CostEstimate(
            flops=2 * flops, bytes_accessed=2 * count * width_x * cells * depth, transcendentals=0
        ),
    )(planes, plane_pad, row_table)


def pack_kernel(own_ref, other_ref, out_ref):
    _, count, width_x, lanes = own_ref.shape
    kept = lanes // 2
    for u in range(count // 4):
        value = own_ref[0, 4 * u : 4 * u + 4].astype(jnp.float32)
        value = value + other_ref[0, 4 * u : 4 * u + 4].astype(jnp.float32)
        value = value.reshape(4 * width_x, lanes)
        stacked = jnp.concatenate([value[:, :kept], value[:, kept:]], axis=0)
        out_ref[:, u * 128 : u * 128 + 128] = stacked.T.astype(jnp.bfloat16)


def pack_call(own, other):
    share, count, width_x, lanes = other.shape
    block = pl.BlockSpec((1, count, width_x, lanes), lambda s: (s, 0, 0, 0))
    kept = lanes // 2
    return pl.pallas_call(
        pack_kernel,
        grid=(share,),
        in_specs=[block, block],
        out_specs=pl.BlockSpec((kept, count * 32), lambda s: (s, 0)),
        out_shape=jax.ShapeDtypeStruct((share * kept, count * 32), jnp.bfloat16),
        compiler_params=params(),
        cost_estimate=pl.CostEstimate(
            flops=other.size, bytes_accessed=other.size * 6, transcendentals=0
        ),
    )(own, other)


def unpack_kernel(in_ref, out_ref):
    _, count, width_x, lanes = out_ref.shape
    for u in range(count // 4):
        value = in_ref[:, u * 128 : u * 128 + 128].astype(jnp.float32).T
        value = jnp.concatenate([value[: 4 * width_x], value[4 * width_x :]], axis=1)
        out_ref[0, 4 * u : 4 * u + 4] = value.reshape(4, width_x, lanes).astype(jnp.bfloat16)


def unpack_call(packed, width_x):
    kept = MS * MT
    share = packed.shape[0] // kept
    count = packed.shape[1] // 32
    return pl.pallas_call(
        unpack_kernel,
        grid=(share,),
        in_specs=[pl.BlockSpec((kept, count * 32), lambda s: (s, 0))],
        out_specs=pl.BlockSpec((1, count, width_x, 2 * kept), lambda s: (s, 0, 0, 0)),
        out_shape=jax.ShapeDtypeStruct((share, count, width_x, 2 * kept), jnp.bfloat16),
        compiler_params=params(),
        cost_estimate=pl.CostEstimate(
            flops=packed.size, bytes_accessed=packed.size * 4, transcendentals=0
        ),
    )(packed)


def gather_modes(in_refs, table_ref, modes_ref):
    span = modes_ref.shape[-1]
    c = 0
    for ref in in_refs:
        sources = ref.shape[0] // span
        for u in range(ref.shape[1] // 128):
            values = jnp.concatenate(
                [ref[g * span : g * span + span, u * 128 : u * 128 + 128] for g in range(sources)],
                axis=1,
            )
            found = lax.dot_general(
                table_ref[...], values, (((1,), (1,)), ((), ())), preferred_element_type=jnp.float32
            )
            found = found.astype(jnp.bfloat16).astype(jnp.float32)
            modes_ref[:, c : c + 4] = found.reshape(2, 4, MS, span)
            c += 4


def scatter_modes(modes_ref, table_ref, out_refs):
    span = modes_ref.shape[-1]
    c = 0
    for ref in out_refs:
        sources = ref.shape[0] // span
        for u in range(ref.shape[1] // 128):
            values = modes_ref[:, c : c + 4].reshape(2 * 4 * MS, span).astype(jnp.bfloat16)
            cells = lax.dot_general(
                values, table_ref[...], (((0,), (0,)), ((), ())), preferred_element_type=jnp.float32
            ).astype(jnp.bfloat16)
            for g in range(sources):
                ref[g * span : g * span + span, u * 128 : u * 128 + 128] = cells[
                    :, g * 128 : g * 128 + 128
                ]
            c += 4


def apply_kernel(pieces, *refs):
    in_refs, (table_ref, weight_ref, modes_ref) = refs[:pieces], refs[pieces : pieces + 3]
    out_refs, mixed_ref = refs[pieces + 3 : -1], refs[-1]
    channels = modes_ref.shape[1]
    step = pl.program_id(0)

    @pl.when(step == 0)
    def _():
        gather_modes(in_refs, table_ref, modes_ref)

    real = jnp.zeros(modes_ref.shape[2:], jnp.float32)
    imag = real
    for i in range(channels):
        real_weight = weight_ref[0, i, 0].astype(jnp.float32)
        imag_weight = weight_ref[1, i, 0].astype(jnp.float32)
        real_mode, imag_mode = modes_ref[0, i], modes_ref[1, i]
        real = real + real_weight * real_mode - imag_weight * imag_mode
        imag = imag + real_weight * imag_mode + imag_weight * real_mode
    mixed_ref[0, step] = real
    mixed_ref[1, step] = imag

    @pl.when(step == channels - 1)
    def _():
        scatter_modes(mixed_ref, table_ref, out_refs)


def apply_call(blocks, table, weight):
    _, channels, _, _, span = weight.shape
    modes = (2, channels, MS, span)
    return pl.pallas_call(
        functools.partial(apply_kernel, len(blocks)),
        grid=(channels,),
        in_specs=[whole(b.shape) for b in blocks]
        + [
            whole(table.shape),
            pl.BlockSpec((2, channels, 1, MS, span), lambda s: (0, 0, s, 0, 0)),
        ],
        out_specs=[whole(modes)] + [whole(b.shape) for b in blocks],
        out_shape=[jax.ShapeDtypeStruct(modes, jnp.float32)]
        + [jax.ShapeDtypeStruct(b.shape, jnp.bfloat16) for b in blocks],
        scratch_shapes=[pltpu.VMEM(modes, jnp.float32)],
        compiler_params=params(),
    )(*blocks, table, weight)


def adjoint_kernel(pieces, *refs):
    in_refs = refs[:pieces]
    table_ref, weight_ref, modes_ref, grad_ref = refs[pieces : pieces + 4]
    out_refs, up_ref, back_ref = refs[pieces + 4 : -2], refs[-2], refs[-1]
    channels = modes_ref.shape[1]
    step = pl.program_id(0)

    @pl.when(step == 0)
    def _():
        gather_modes(in_refs, table_ref, up_ref)

    real_mode, imag_mode = modes_ref[0, step], modes_ref[1, step]
    real = jnp.zeros(modes_ref.shape[2:], jnp.float32)
    imag = real
    for o in range(channels):
        real_up, imag_up = up_ref[0, o], up_ref[1, o]
        grad_ref[0, 0, o] = real_up * real_mode + imag_up * imag_mode
        grad_ref[1, 0, o] = imag_up * real_mode - real_up * imag_mode
        real_weight = weight_ref[0, 0, o].astype(jnp.float32)
        imag_weight = weight_ref[1, 0, o].astype(jnp.float32)
        real = real + real_weight * real_up + imag_weight * imag_up
        imag = imag + real_weight * imag_up - imag_weight * real_up
    back_ref[0, step] = real
    back_ref[1, step] = imag

    @pl.when(step == channels - 1)
    def _():
        scatter_modes(back_ref, table_ref, out_refs)


def adjoint_call(blocks, table, weight, modes):
    _, channels, _, _, span = weight.shape
    spec = pl.BlockSpec((2, 1, channels, MS, span), lambda s: (0, s, 0, 0, 0))
    return pl.pallas_call(
        functools.partial(adjoint_kernel, len(blocks)),
        grid=(channels,),
        in_specs=[whole(b.shape) for b in blocks] + [whole(table.shape), spec, whole(modes.shape)],
        out_specs=[spec] + [whole(b.shape) for b in blocks],
        out_shape=[jax.ShapeDtypeStruct(weight.shape, jnp.float32)]
        + [jax.ShapeDtypeStruct(b.shape, jnp.bfloat16) for b in blocks],
        scratch_shapes=[pltpu.VMEM(modes.shape, jnp.float32)] * 2,
        compiler_params=params(),
    )(*blocks, table, weight, modes)


def cells_kernel(counts, with_slope, *refs):
    pieces = 4 * len(counts)
    mode_refs, (row_ref, plane_ref, mix_ref, planes_ref) = refs[:pieces], refs[pieces : pieces + 4]
    rest, out_ref, cell_ref = refs[pieces + 4 : -2], refs[-2], refs[-1]
    channels, _, tall, depth = planes_ref.shape
    kept = MS * MT
    step = pl.program_id(0)
    cells = row_ref.shape[0] // 8

    @pl.when(step == 0)
    def _():
        first = 0
        for at, count in enumerate(counts):
            refs_of = mode_refs[4 * at : 4 * at + 4]

            def body(c, carry, first=first, refs_of=refs_of):
                value = jnp.concatenate([ref[:, c] for ref in refs_of], axis=0).astype(jnp.float32)
                for g in range(value.shape[1] // 8):
                    part = value[:, g * 8 : g * 8 + 8].reshape(MS * 8, 2 * kept)
                    turned = jnp.concatenate([-part[:, kept:], part[:, :kept]], axis=1)
                    both = jnp.concatenate([part, turned], axis=0).astype(jnp.bfloat16)
                    cell_ref[g, first + c] = jnp.dot(
                        row_ref[...], both, preferred_element_type=jnp.float32
                    ).astype(jnp.bfloat16)
                return carry

            lax.fori_loop(0, count, body, 0)
            first += count

    parts = cells // tall
    x = step // parts
    row = pl.multiple_of((x % 8) * cells + (step % parts) * tall, tall)
    modes = cell_ref[x // 8, :, pl.ds(row, tall), :].reshape(channels * tall, 2 * kept)
    planes = planes_ref[...].reshape(channels * tall, depth)
    value = jnp.dot(modes, plane_ref[...], preferred_element_type=jnp.float32)
    value = value + jnp.dot(mix_ref[...], planes, preferred_element_type=jnp.float32)
    if with_slope:
        cot_ref, bias_ref = rest
        value = value + bias_ref[...]
        cot = cot_ref[...].reshape(channels * tall, depth).astype(jnp.float32)
        value = cot * gelu_slope(value)
    out_ref[...] = value.astype(jnp.bfloat16).reshape(out_ref.shape)


def cells_call(pieces, row_table, plane_back, mix, planes, cotangent=None, bias=None):
    channels, width_x, cells, depth = planes.shape
    kept = MS * MT
    tall = 16
    parts = cells // tall
    counts = tuple(group[0].shape[1] for group in pieces)
    flat = [p for group in pieces for p in group]
    spec = pl.BlockSpec((channels, 1, tall, depth), lambda s: (0, s // parts, s % parts, 0))
    extra = [] if bias is None else [cotangent, jnp.repeat(bias, tall)[:, None]]
    extra_specs = [] if bias is None else [spec, whole((channels * tall, 1))]
    mixing = (mix[:, None, :, None] * jnp.eye(tall, dtype=mix.dtype)[None, :, None, :]).reshape(
        channels * tall, channels * tall
    )
    return pl.pallas_call(
        functools.partial(cells_kernel, counts, bias is not None),
        grid=(width_x * parts,),
        in_specs=[whole(p.shape) for p in flat]
        + [whole(row_table.shape), whole(plane_back.shape), whole(mixing.shape), spec]
        + extra_specs,
        out_specs=spec,
        out_shape=jax.ShapeDtypeStruct(planes.shape, jnp.bfloat16),
        scratch_shapes=[
            pltpu.VMEM((width_x // 8, channels, 8 * cells, 2 * kept), jnp.bfloat16)
        ],
        compiler_params=params(),
    )(*flat, row_table, plane_back, mixing, planes, *extra)


def local_kernels(field, cotangent, spectral_weight, local_weight, bias):
    channels, width_x, cells, depth = field.shape
    gx_size = NX // width_x
    kept = MS * MT
    plane_table = plane_tables(NZ, NT, MS, MT)
    gap = jnp.zeros((depth, 256 - kept), jnp.bfloat16)
    plane_pad = jnp.concatenate([plane_table[:, :kept], gap, plane_table[:, kept:], gap], axis=1)
    plane_back = plane_table.T
    row_table, across_table = kernel_tables(width_x, gx_size)
    row_back = row_table.T
    chunks = ((0, 8), (8, channels - 8))
    other_core = [(d, d ^ 1) for d in range(4)]
    other_y = [(d, d ^ 2) for d in range(4)]

    def forward_chain(planes):
        sent = []
        for first, count in chunks:
            near, far = rows_call(planes, first, count, plane_pad, row_table)
            near = near + lax.ppermute(far, "gy", other_core)
            sent.append((near, lax.ppermute(near[MS // 4 :], "gy", other_y)))
        blocks = []
        for near, other in sent:
            packed = pack_call(near, other)
            blocks.append(lax.all_to_all(packed, "gx", split_axis=0, concat_axis=0, tiled=True))
        return blocks

    def inverse_chain(blocks):
        pieces = []
        for block in blocks:
            moved = lax.all_to_all(block, "gx", split_axis=0, concat_axis=0, tiled=True)
            own = unpack_call(moved, width_x)
            beside = lax.ppermute(own, "gy", other_y)
            pieces.append(
                [
                    own,
                    beside,
                    lax.ppermute(own, "gy", other_core),
                    lax.ppermute(beside, "gy", other_core),
                ]
            )
        return pieces

    modes, *mixed = apply_call(forward_chain(field), across_table, spectral_weight)
    upstream = cells_call(
        inverse_chain(mixed), row_back, plane_back, local_weight.T, field, cotangent, bias
    )
    grad_weight, *back = adjoint_call(
        forward_chain(upstream), across_table, spectral_weight, modes
    )
    result = cells_call(inverse_chain(back), row_back, plane_back, local_weight, upstream)
    return (result, grad_weight)


def solution(mesh):
    in_specs = (
        P(None, "gx", "gy", None),
        P(None, "gx", "gy", None),
        P(None, None, None, None, ("gy", "gx")),
        P(),
        P(),
    )
    out_specs = (P(None, "gx", "gy", None), P(None, None, None, None, ("gy", "gx")))
    width_x, four_rows = NX // mesh.shape["gx"], mesh.shape["gy"] == 4
    body = local_kernels if four_rows and width_x == 16 else local
    return jax.shard_map(body, mesh=mesh, in_specs=in_specs, out_specs=out_specs, check_vma=False)
```
